32 devices in a mesh: batch: 4 (over y, x), group: 8 (over z, core).
Axes of the slice: x: 2, y: 2, z: 4, core: 2. Of those that a mesh axis runs over, the one named last changes fastest.
Arguments:
- noise: bfloat16 [512, 99840], P('batch', 'group'), may hold values from -24 to 24
- data: bfloat16 [512, 99840], P('batch', 'group'), may hold values from -6 to 6
Outputs:
- targets: bfloat16 [512, 99840], P('batch', 'group')
- potential: float32 [512], replicated
The draws below stay inside these ranges and needn't reach their ends.
All inputs are finite; a program needn't handle non-finite values.
Results may differ from the reference program's by a relative error of at most 0.007.
Values may be sent and summed in bfloat16 or wider, within the bound.
No kernel may reach another device: no remote copies, remote signals or barrier semaphores. Data moves between devices by JAX's collectives and lax.ppermute only.
A program may use at most 64 MiB of HBM per device.

```python
import jax
import jax.numpy as jnp
from jax import lax

ITERS = 4
FEAT = 99840
BATCH = 512


def draw_noise(key, part):
    key = jax.random.fold_in(key, 11)
    row_key, value_key = jax.random.split(key, 2)
    picks = jax.random.randint(row_key, (BATCH,), 0, 8)
    rows_index = jnp.arange(BATCH)
    scaled = jnp.logical_or(picks == 0, rows_index == 0)
    factor = jnp.where(scaled, 4.0, 1.0).astype(jnp.float32)
    values = jnp.clip(jax.random.normal(value_key, (BATCH, FEAT), jnp.float32), -6.0, 6.0)
    return (values * factor[:, None]).astype(jnp.bfloat16)


def block_scale(stream_key, extent, pieces, least, largest):
    level = 1.0
    for dim, blocks in pieces:
        draws = jax.random.uniform(jax.random.fold_in(jax.random.fold_in(stream_key, 6), dim), (blocks,), jnp.float32, least / len(pieces), largest / len(pieces))
        level = level * jnp.repeat(jnp.exp(draws), extent[dim] // blocks).reshape((-1,) + (1,) * (len(extent) - 1 - dim))
    return level


def bell_draw(own_key, shape, scale, limit, cuts=(), held_as=jnp.bfloat16):
    gain = block_scale(own_key, shape, cuts, -0.22, 0.18) if cuts else 1.0
    drawn = jax.random.normal(own_key, shape, jnp.float32) * scale * gain
    return jnp.minimum(jnp.maximum(drawn, -limit), limit).astype(held_as)


def setup_inputs(seed: int = 0) -> dict:
    seeds = jax.random.split(jax.random.key(seed), 3)
    noise = draw_noise(jax.random.fold_in(seeds[2], 71), 0)
    data = bell_draw(seeds[1], (BATCH, FEAT), 1.0, 6.0, ((0, 4), (1, 8)))
    return {"noise": noise, "data": data}


def log_sum(values, axis):
    top = lax.optimization_barrier(jnp.max(values, axis=axis, keepdims=True))
    return jnp.squeeze(top, axis) + jnp.log(lax.optimization_barrier(jnp.sum(jnp.exp(values - top), axis=axis)))

def reference(noise, data):
    eps = 2.0 / jnp.sqrt(jnp.float32(FEAT))
    loga = -jnp.log(jnp.float32(BATCH))
    noise_sq = lax.optimization_barrier(jnp.sum(jnp.square(noise.astype(jnp.float32)), axis=1))
    data_sq = lax.optimization_barrier(jnp.sum(jnp.square(data.astype(jnp.float32)), axis=1))
    cross = jnp.dot(noise, data.T, preferred_element_type=jnp.float32)
    cost = (noise_sq[:, None] + data_sq[None, :] - 2.0 * cross) / jnp.float32(FEAT)
    potential = jnp.zeros((BATCH,), jnp.float32)
    for step in range(ITERS):
        rowpot = eps * loga - eps * log_sum((potential[None, :] - cost) / eps, 1)
        potential = eps * loga - eps * log_sum((rowpot[:, None] - cost) / eps, 0)
    scores = (potential[None, :] - cost) / eps
    weights = jnp.exp(scores - log_sum(scores, 1)[:, None]).astype(jnp.bfloat16)
    targets = jnp.dot(weights, data, preferred_element_type=jnp.float32).astype(jnp.bfloat16)
    return (targets, potential)
```

```python
import functools

import jax
import jax.numpy as jnp
from jax import lax
from jax.experimental import pallas as pl
from jax.experimental.pallas import tpu as pltpu
from jax.sharding import PartitionSpec as P

ITERS = 4
FEAT = 99840


def combined_all(value, axis, join):
    pieces = jax.tree.map(lambda part: lax.all_gather(part, axis), value)
    head = jax.tree.map(lambda part: part[0], pieces)
    tail = jax.tree.map(lambda part: part[1:], pieces)
    total, _ = lax.scan(lambda total, slab: (join(total, slab), None), head, tail)
    return total


def combine_parts(first, second):
    top = jnp.maximum(first[0], second[0])
    total = first[1] * jnp.exp(first[0] - top) + second[1] * jnp.exp(second[0] - top)
    return (top, total)


def local_parts(values, axis):
    top = jnp.max(values, axis=axis)
    total = jnp.sum(jnp.exp(values - jnp.expand_dims(top, axis)), axis=axis)
    return (top, total)


def local_any(noise, data):
    eps = 2.0 / jnp.sqrt(jnp.float32(FEAT))
    batch_total = noise.shape[0] * lax.axis_size("batch")
    loga = -jnp.log(jnp.float32(batch_total))
    noise_sq = jnp.sum(jnp.square(noise.astype(jnp.float32)), axis=1)
    all_rows = lax.all_gather(data, "batch", axis=0, tiled=True)
    piece_sq = jnp.sum(jnp.square(all_rows.astype(jnp.float32)), axis=1)
    cross = lax.dot_general(
        noise, all_rows, (((1,), (1,)), ((), ())), preferred_element_type=jnp.float32
    )
    partial_value = noise_sq[:, None] + piece_sq[None, :] - 2.0 * cross
    cost = lax.psum(partial_value, "group") / jnp.float32(FEAT)
    potential = jnp.zeros((batch_total,), jnp.float32)
    for step in range(ITERS):
        top, total = local_parts((potential[None, :] - cost) / eps, 1)
        rowpot = eps * loga - eps * (top + jnp.log(total))
        parts = local_parts((rowpot[:, None] - cost) / eps, 0)
        top, total = combined_all(parts, "batch", combine_parts)
        potential = eps * loga - eps * (top + jnp.log(total))
    scores = (potential[None, :] - cost) / eps
    top, total = local_parts(scores, 1)
    weights = jnp.exp(scores - (top + jnp.log(total))[:, None]).astype(jnp.bfloat16)
    targets = jnp.dot(weights, all_rows, preferred_element_type=jnp.float32)
    return (targets.astype(jnp.bfloat16), potential)


X, Y, DIAG = 1, 2, 3


def swap(value, way):
    return lax.ppermute(value, "batch", [(i, i ^ way) for i in range(4)])


VMEM = pl.BlockSpec(memory_space=pltpu.VMEM)
SMEM = pl.BlockSpec(memory_space=pltpu.SMEM)
HBM = pl.BlockSpec(memory_space=pltpu.HBM)


def split_kernel(whole_ref, low_ref, high_ref, sem):
    size = low_ref.shape[0]
    copies = [
        pltpu.make_async_copy(whole_ref.at[pl.ds(0, size), :], low_ref, sem.at[0]),
        pltpu.make_async_copy(whole_ref.at[pl.ds(size, high_ref.shape[0]), :], high_ref, sem.at[1]),
    ]
    for copy in copies:
        copy.start()
    for copy in copies:
        copy.wait()


def split(whole, size):
    feats, rows = whole.shape
    return pl.pallas_call(
        split_kernel,
        out_shape=(
            jax.ShapeDtypeStruct((size, rows), whole.dtype),
            jax.ShapeDtypeStruct((feats - size, rows), whole.dtype),
        ),
        in_specs=[HBM],
        out_specs=(VMEM, VMEM),
        scratch_shapes=[pltpu.SemaphoreType.DMA((2,))],
        cost_estimate=pl.CostEstimate(flops=0, bytes_accessed=4 * whole.size, transcendentals=0),
    )(whole)


DEPTH = 512


def cross_kernel(spans, noise_ref, *refs):
    *refs, out_ref = refs
    width = noise_ref.shape[0]

    def add(piece_ref, start, at, size, total):
        cross, square = total
        piece = piece_ref[pl.ds(at, size), :]
        noise = noise_ref[:, pl.ds(start + at, size)]
        cross = cross + jnp.dot(noise, piece, preferred_element_type=jnp.float32)
        value = jnp.square(piece.astype(jnp.float32))
        return cross, square + jnp.sum(value.reshape(size // 8, 8, width), axis=0)

    for k, block_spans in enumerate(spans):
        (prior_ref, *pieces), refs = refs[: 1 + len(block_spans)], refs[1 + len(block_spans):]
        total = (jnp.zeros((width, width), jnp.float32), jnp.zeros((8, width), jnp.float32))
        for (start, size), piece_ref in zip(block_spans, pieces):
            whole = size // DEPTH

            def step(t, total):
                return add(piece_ref, start, pl.multiple_of(t * DEPTH, DEPTH), DEPTH, total)

            total = lax.fori_loop(0, whole, step, total, unroll=2)
            if size % DEPTH:
                total = add(piece_ref, start, whole * DEPTH, size % DEPTH, total)
        cross, square = total
        out_ref[:, k * width : (k + 1) * width] = prior_ref[...] + (
            jnp.sum(square, axis=0, keepdims=True) - 2.0 * cross
        )


def crossed(noise, *blocks):
    rows = noise.shape[0]
    spans = [block[2::2] for block in blocks]
    values = [value for block in blocks for value in (block[0],) + block[1::2]]
    flops = sum(2 * rows * rows * size for block_spans in spans for _, size in block_spans)
    return pl.pallas_call(
        functools.partial(cross_kernel, spans),
        out_shape=jax.ShapeDtypeStruct((rows, rows * len(blocks)), jnp.float32),
        in_specs=[VMEM] * (1 + len(values)),
        out_specs=VMEM,
        compiler_params=pltpu.CompilerParams(vmem_limit_bytes=16 * 2**20),
        cost_estimate=pl.CostEstimate(flops=flops, bytes_accessed=flops // 64, transcendentals=0),
    )(noise, *values)


STEP = 64
TILES = 10


def pair_kernel(rows, feats, places, own_ref, *refs):
    early_refs, late_refs, refs = refs[:4], refs[4:8], refs[8:]
    pieces, refs = refs[: len(places)], refs[len(places):]
    targets_ref, potential_ref, blocks, held, scores, out, in_sem, out_sem = refs
    batch = 4 * rows
    eps = 2.0 / FEAT**0.5
    scale = -1.0 / (FEAT * eps)
    loga = -jnp.log(jnp.float32(batch))
    own = own_ref[0]

    loads = []
    for k, (start, r) in enumerate(places):
        copy = pltpu.make_async_copy(
            pieces[k],
            held.at[pl.ds(start, pieces[k].shape[0]), pl.ds(r * rows, rows)],
            in_sem.at[k],
        )
        copy.start()
        loads.append(copy)

    def block(i):
        return pl.ds(pl.multiple_of(i * rows, rows), rows)

    for p in range(4):
        for r in range(DIAG):
            blocks[block(own ^ p), block(own ^ (p ^ r))] = early_refs[p][:, block(r)] * scale
        blocks[block(own ^ p), block(own ^ (p ^ DIAG))] = late_refs[p][...] * scale

    def sweep(_, v):
        u = []
        top = jnp.full((1, batch), -jnp.inf, jnp.float32)
        for c in range(batch // STEP):
            k = blocks[pl.ds(c * STEP, STEP), :]
            a = k + v
            m = jnp.max(a, axis=1, keepdims=True)
            s = jnp.sum(jnp.exp(a - m), axis=1, keepdims=True)
            u.append(loga - (m + jnp.log(s)))
            top = jnp.maximum(top, jnp.max(k + u[-1], axis=0, keepdims=True))
        total = jnp.zeros((1, batch), jnp.float32)
        for c in range(batch // STEP):
            a = blocks[pl.ds(c * STEP, STEP), :] + u[c]
            total = total + jnp.sum(jnp.exp(a - top), axis=0, keepdims=True)
        return loga - (top + jnp.log(total))

    v = lax.fori_loop(0, ITERS, sweep, jnp.zeros((1, batch), jnp.float32))
    potential_ref[...] = v * eps

    a = blocks[block(own), :] + v
    m = jnp.max(a, axis=1, keepdims=True)
    s = jnp.sum(jnp.exp(a - m), axis=1, keepdims=True)
    scores[...] = jnp.exp(a - (m + jnp.log(s)))
    w = jnp.concatenate([scores[:, block(own ^ r)].T for r in range(4)], axis=0).astype(jnp.bfloat16)
    for copy in loads:
        copy.wait()

    tile = feats // TILES

    def stored(t):
        part = pl.ds(pl.multiple_of(t * tile, 16), tile)
        return pltpu.make_async_copy(out.at[part, :], targets_ref.at[part, :], out_sem.at[t])

    def multiply(t, _):
        part = pl.ds(pl.multiple_of(t * tile, 16), tile)
        out[part, :] = jnp.dot(held[part, :], w, preferred_element_type=jnp.float32).astype(jnp.bfloat16)
        stored(t).start()
        return 0

    lax.fori_loop(0, TILES, multiply, 0)
    for t in range(TILES):
        stored(t).wait()


def paired(own, early, late, pieces, places, rows, feats):
    batch = 4 * rows
    return pl.pallas_call(
        functools.partial(pair_kernel, rows, feats, places),
        out_shape=(
            jax.ShapeDtypeStruct((feats, rows), jnp.bfloat16),
            jax.ShapeDtypeStruct((1, batch), jnp.float32),
        ),
        in_specs=[SMEM] + [VMEM] * 8 + [HBM] * len(pieces),
        out_specs=(HBM, VMEM),
        scratch_shapes=[
            pltpu.VMEM((batch, batch), jnp.float32),
            pltpu.VMEM((feats, batch), jnp.bfloat16),
            pltpu.VMEM((rows, batch), jnp.float32),
            pltpu.VMEM((feats, rows), jnp.bfloat16),
            pltpu.SemaphoreType.DMA((len(pieces),)),
            pltpu.SemaphoreType.DMA((TILES,)),
        ],
        compiler_params=pltpu.CompilerParams(vmem_limit_bytes=58 * 2**20),
        cost_estimate=pl.CostEstimate(
            flops=2 * rows * batch * feats, bytes_accessed=10 * rows * feats, transcendentals=9 * batch * batch
        ),
    )(own, *early, *late, *pieces)


def squared(values_t):
    return jnp.sum(jnp.square(values_t.astype(jnp.float32)), axis=0)


def group_sum(partial_value):
    groups = lax.axis_size("group")
    rows, width = partial_value.shape
    parts = lax.all_to_all(partial_value, "group", 0, 0, tiled=True)
    return jnp.sum(parts.reshape(groups, rows // groups, width), axis=0)


def to_all(mine, axes, devices):
    copies = jnp.broadcast_to(mine[None], (devices,) + mine.shape)
    held = lax.all_to_all(copies, axes, 0, 0, tiled=True)
    return held.reshape(devices * mine.shape[0], mine.shape[1])


def local_square(noise, data):
    rows, feats = noise.shape
    groups = lax.axis_size("group")
    noise_t, data_t = noise.T, data.T
    own = lax.axis_index("batch").astype(jnp.int32).reshape(1)

    half = feats // 256 * 128
    low, high = (0, half), (half, feats - half)
    d_low, d_high = split(data_t, half)
    x_high, y_low = swap(d_high, X), swap(d_low, Y)
    x_low, y_high = swap(d_low, X), swap(d_high, Y)
    diag_low, diag_high = swap(y_low, X), swap(x_high, Y)

    start = jnp.broadcast_to(squared(noise_t)[:, None], (rows, rows))
    early = crossed(
        noise,
        (crossed(noise, (start, d_low, low, d_high, high)),),
        (crossed(noise, (start, x_high, high)), x_low, low),
        (crossed(noise, (start, y_low, low)), y_high, high),
    )
    early_own = to_all(group_sum(early), "group", groups)
    early_rows = [early_own, swap(early_own, X), swap(early_own, Y), swap(early_own, DIAG)]
    early_rows[0], diag_low, diag_high = lax.optimization_barrier((early_own, diag_low, diag_high))
    late = crossed(noise, (start, diag_low, low, diag_high, high))
    way = 1
    while way < groups:
        late = late + lax.ppermute(late, "group", [(g, g ^ way) for g in range(groups)])
        way *= 2
    late_rows = [late, swap(late, X), swap(late, Y), swap(late, DIAG)]

    pieces = [d_low, d_high, x_low, x_high, y_low, y_high, diag_low, diag_high]
    places = [(span[0], r) for r in range(4) for span in (low, high)]
    targets_t, potential = paired(own, early_rows, late_rows, pieces, places, rows, feats)
    return (targets_t.T, potential[0])


def solution(mesh):
    in_specs = (P("batch", "group"), P("batch", "group"))
    out_specs = (P("batch", "group"), P())
    groups = mesh.shape["group"]
    paired_form = mesh.shape["batch"] == 4 and groups & (groups - 1) == 0
    local = local_square if paired_form else local_any
    return jax.shard_map(local, mesh=mesh, in_specs=in_specs, out_specs=out_specs, check_vma=False)
```

```python
import functools

import jax
import jax.numpy as jnp
from jax import lax
from jax.experimental import pallas as pl
from jax.experimental.pallas import tpu as pltpu
from jax.sharding import PartitionSpec as P

ITERS = 4
FEAT = 99840


def combined_all(value, axis, join):
    pieces = jax.tree.map(lambda part: lax.all_gather(part, axis), value)
    head = jax.tree.map(lambda part: part[0], pieces)
    tail = jax.tree.map(lambda part: part[1:], pieces)
    total, _ = lax.scan(lambda total, slab: (join(total, slab), None), head, tail)
    return total


def combine_parts(first, second):
    top = jnp.maximum(first[0], second[0])
    total = first[1] * jnp.exp(first[0] - top) + second[1] * jnp.exp(second[0] - top)
    return (top, total)


def local_parts(values, axis):
    top = jnp.max(values, axis=axis)
    total = jnp.sum(jnp.exp(values - jnp.expand_dims(top, axis)), axis=axis)
    return (top, total)


def local_any(noise, data):
    eps = 2.0 / jnp.sqrt(jnp.float32(FEAT))
    batch_total = noise.shape[0] * lax.axis_size("batch")
    loga = -jnp.log(jnp.float32(batch_total))
    noise_sq = jnp.sum(jnp.square(noise.astype(jnp.float32)), axis=1)
    all_rows = lax.all_gather(data, "batch", axis=0, tiled=True)
    piece_sq = jnp.sum(jnp.square(all_rows.astype(jnp.float32)), axis=1)
    cross = lax.dot_general(
        noise, all_rows, (((1,), (1,)), ((), ())), preferred_element_type=jnp.float32
    )
    partial_value = noise_sq[:, None] + piece_sq[None, :] - 2.0 * cross
    cost = lax.psum(partial_value, "group") / jnp.float32(FEAT)
    potential = jnp.zeros((batch_total,), jnp.float32)
    for step in range(ITERS):
        top, total = local_parts((potential[None, :] - cost) / eps, 1)
        rowpot = eps * loga - eps * (top + jnp.log(total))
        parts = local_parts((rowpot[:, None] - cost) / eps, 0)
        top, total = combined_all(parts, "batch", combine_parts)
        potential = eps * loga - eps * (top + jnp.log(total))
    scores = (potential[None, :] - cost) / eps
    top, total = local_parts(scores, 1)
    weights = jnp.exp(scores - (top + jnp.log(total))[:, None]).astype(jnp.bfloat16)
    targets = jnp.dot(weights, all_rows, preferred_element_type=jnp.float32)
    return (targets.astype(jnp.bfloat16), potential)


X, Y, DIAG = 1, 2, 3


def swap(value, way):
    return lax.ppermute(value, "batch", [(i, i ^ way) for i in range(4)])


VMEM = pl.BlockSpec(memory_space=pltpu.VMEM)
SMEM = pl.BlockSpec(memory_space=pltpu.SMEM)
HBM = pl.BlockSpec(memory_space=pltpu.HBM)


PARTS = 4


def cross_kernel(spans, noise_ref, *refs):
    *refs, out_ref = refs
    width = noise_ref.shape[0]
    for k, block_spans in enumerate(spans):
        (prior_ref, *pieces), refs = refs[: 1 + len(block_spans)], refs[1 + len(block_spans):]
        total = prior_ref[...]
        for (start, size), piece_ref in zip(block_spans, pieces):
            step = -(-size // (PARTS * 128)) * 128
            sums = []
            for at in range(0, size, step):
                deep = min(step, size - at)
                piece = piece_ref[at : at + deep, :]
                noise = noise_ref[:, start + at : start + at + deep]
                cross = jnp.dot(noise, piece, preferred_element_type=jnp.float32)
                square = jnp.sum(jnp.square(piece.astype(jnp.float32)), axis=0, keepdims=True)
                sums.append(square - 2.0 * cross)
            total = total + functools.reduce(lambda first, second: first + second, sums)
        out_ref[:, k * width : (k + 1) * width] = total


def crossed(noise, *blocks):
    rows = noise.shape[0]
    spans = [block[2::2] for block in blocks]
    values = [value for block in blocks for value in (block[0],) + block[1::2]]
    flops = sum(2 * rows * rows * size for block_spans in spans for _, size in block_spans)
    return pl.pallas_call(
        functools.partial(cross_kernel, spans),
        out_shape=jax.ShapeDtypeStruct((rows, rows * len(blocks)), jnp.float32),
        in_specs=[VMEM] * (1 + len(values)),
        out_specs=VMEM,
        compiler_params=pltpu.CompilerParams(vmem_limit_bytes=16 * 2**20),
        cost_estimate=pl.CostEstimate(flops=flops, bytes_accessed=flops // 64, transcendentals=0),
    )(noise, *values)


STEP = 64
TILES = 5


def pair_kernel(rows, feats, places, index_ref, *refs):
    early_refs, late_refs, refs = (refs[:4], refs[4:8]), refs[8:10], refs[10:]
    pieces, refs = refs[: len(places)], refs[len(places):]
    targets_ref, potential_ref, blocks, held, scores, out, in_sem, out_sem = refs
    batch = 4 * rows
    eps = 2.0 / FEAT**0.5
    scale = -1.0 / (FEAT * eps)
    loga = -jnp.log(jnp.float32(batch))
    own, core = index_ref[0], index_ref[1]
    half = rows // 2

    loads = []
    for k, (start, r) in enumerate(places):
        copy = pltpu.make_async_copy(
            pieces[k],
            held.at[pl.ds(start, pieces[k].shape[0]), pl.ds(r * rows, rows)],
            in_sem.at[k],
        )
        copy.start()
        loads.append(copy)

    def block(i):
        return pl.ds(pl.multiple_of(i * rows, rows), rows)

    for p in range(4):
        for side in range(2):
            part = pl.ds(p * half, half)
            into = pl.ds(pl.multiple_of((own ^ p) * rows + (core ^ side) * half, half), half)
            for r in range(DIAG):
                blocks[into, block(own ^ (p ^ r))] = early_refs[side][p][:, block(r)] * scale
            blocks[into, block(own ^ (p ^ DIAG))] = late_refs[side][part, :] * scale

    def sweep(_, v):
        u = []
        top = jnp.full((1, batch), -jnp.inf, jnp.float32)
        for c in range(batch // STEP):
            k = blocks[pl.ds(c * STEP, STEP), :]
            a = k + v
            m = jnp.max(a, axis=1, keepdims=True)
            s = jnp.sum(jnp.exp(a - m), axis=1, keepdims=True)
            u.append(loga - (m + jnp.log(s)))
            top = jnp.maximum(top, jnp.max(k + u[-1], axis=0, keepdims=True))
        total = jnp.zeros((1, batch), jnp.float32)
        for c in range(batch // STEP):
            a = blocks[pl.ds(c * STEP, STEP), :] + u[c]
            total = total + jnp.sum(jnp.exp(a - top), axis=0, keepdims=True)
        return loga - (top + jnp.log(total))

    v = lax.fori_loop(0, ITERS, sweep, jnp.zeros((1, batch), jnp.float32))
    potential_ref[...] = v * eps

    a = blocks[block(own), :] + v
    m = jnp.max(a, axis=1, keepdims=True)
    s = jnp.sum(jnp.exp(a - m), axis=1, keepdims=True)
    scores[...] = jnp.exp(a - (m + jnp.log(s)))
    w = jnp.concatenate([scores[:, block(own ^ r)].T for r in range(4)], axis=0).astype(jnp.bfloat16)
    tile = feats // TILES

    def stored(t):
        part = pl.ds(pl.multiple_of(t * tile, 16), tile)
        return pltpu.make_async_copy(out.at[part, :], targets_ref.at[part, :], out_sem.at[t])

    def multiply(t, _):
        part = pl.ds(pl.multiple_of(t * tile, 16), tile)
        out[part, :] = jnp.dot(held[part, :], w, preferred_element_type=jnp.float32).astype(jnp.bfloat16)
        stored(t).start()
        return 0

    later = max(start for start, _ in places)
    for copy, (start, _) in zip(loads, places):
        if start < later:
            copy.wait()
    lax.fori_loop(0, later // tile, multiply, 0)
    for copy, (start, _) in zip(loads, places):
        if start >= later:
            copy.wait()
    lax.fori_loop(later // tile, TILES, multiply, 0)
    for t in range(TILES):
        stored(t).wait()


def paired(index, early, late, pieces, places, rows, feats):
    batch = 4 * rows
    return pl.pallas_call(
        functools.partial(pair_kernel, rows, feats, places),
        out_shape=(
            jax.ShapeDtypeStruct((feats, rows), jnp.bfloat16),
            jax.ShapeDtypeStruct((1, batch), jnp.float32),
        ),
        in_specs=[SMEM] + [VMEM] * 10 + [HBM] * len(pieces),
        out_specs=(HBM, VMEM),
        scratch_shapes=[
            pltpu.VMEM((batch, batch), jnp.float32),
            pltpu.VMEM((feats, batch), jnp.bfloat16),
            pltpu.VMEM((rows, batch), jnp.float32),
            pltpu.VMEM((feats, rows), jnp.bfloat16),
            pltpu.SemaphoreType.DMA((len(pieces),)),
            pltpu.SemaphoreType.DMA((TILES,)),
        ],
        compiler_params=pltpu.CompilerParams(vmem_limit_bytes=24 * 2**20),
        cost_estimate=pl.CostEstimate(
            flops=2 * rows * batch * feats, bytes_accessed=10 * rows * feats, transcendentals=9 * batch * batch
        ),
    )(index, *early, *late, *pieces)


def squared(values_t):
    return jnp.sum(jnp.square(values_t.astype(jnp.float32)), axis=0)


def turn(value, way):
    groups = lax.axis_size("group")
    return lax.ppermute(value, "group", [(g, g ^ way) for g in range(groups)])


def core_share(value, core):
    half = value.shape[0] // 2
    kept = lax.dynamic_slice_in_dim(value, core * jnp.uint32(half), half)
    given = lax.dynamic_slice_in_dim(value, (1 - core) * jnp.uint32(half), half)
    return kept + turn(given, 1)


def line_sum(value):
    ways = range(2, lax.axis_size("group"), 2)
    terms = [value] + [turn(value, way) for way in ways]
    while len(terms) > 1:
        terms = [first + second for first, second in zip(terms[::2], terms[1::2])]
    return terms[0]


def group_share(value):
    groups = lax.axis_size("group")
    rows, width = value.shape
    share = rows // groups
    parts = value.reshape(2, groups // 2, share, width).transpose(1, 0, 2, 3).reshape(rows, width)
    parts = lax.all_to_all(parts, "group", 0, 0, tiled=True)
    return jnp.sum(parts.reshape(groups, share, width), axis=0)


def line_gather(value, place):
    lines = lax.axis_size("group") // 2
    shares = jnp.stack([value] + [turn(value, 2 * way) for way in range(1, lines)])
    return jnp.concatenate(
        [lax.dynamic_index_in_dim(shares, place ^ jnp.uint32(z), keepdims=False) for z in range(lines)]
    )


def batch_swaps(value):
    return [value, swap(value, X), swap(value, Y), swap(value, DIAG)]


def local_square(noise, data):
    rows, feats = noise.shape
    noise_t, data_t = noise.T, data.T
    own, group = lax.axis_index("batch"), lax.axis_index("group").astype(jnp.uint32)
    core, line = group & 1, group >> 1
    index = jnp.stack([own.astype(jnp.int32), core.astype(jnp.int32)])

    first = feats * 8 // (15 * 128) * 128
    low, high = (0, first), (first, feats - first)
    d_low, d_high = data_t[:first], data_t[first:]
    x_all, y_low, y_high = swap(data_t, X), swap(d_low, Y), swap(d_high, Y)
    start = jnp.broadcast_to(squared(noise_t)[:, None], (rows, rows))
    own_cost = crossed(noise, (start, d_low, low, d_high, high))
    y_cost = crossed(noise, (start, y_low, low))
    y_low, own_cost, y_cost = lax.optimization_barrier((y_low, own_cost, y_cost))
    diag_low = swap(y_low, X)
    x_tail = x_all[first:]
    diag_high = swap(x_tail, Y)
    x_all, y_high, x_tail = lax.optimization_barrier((x_all, y_high, x_tail))
    early = crossed(noise, (own_cost,), (start, x_all, (0, feats)), (y_cost, y_high, high))
    early_half = line_gather(group_share(early), line)
    early_mine = batch_swaps(early_half)
    _, diag_low = lax.optimization_barrier((early_half, diag_low))
    late = crossed(noise, (start, diag_low, low))
    _, diag_high = lax.optimization_barrier((early_half, diag_high))
    late = crossed(noise, (late, diag_high, high))
    late, *early_mine = lax.optimization_barrier((late, *early_mine))
    early_rows = early_mine + [turn(value, 1) for value in early_mine]
    late_half = core_share(late, core)
    late_half, *early_rows = lax.optimization_barrier((late_half, *early_rows))
    late_half = line_sum(late_half)
    late_mine = jnp.concatenate(batch_swaps(late_half))
    late_rows = [late_mine, turn(late_mine, 1)]

    pieces = [d_low, x_all, y_low, diag_low, d_high, y_high, diag_high]
    places = [(0, 0), (0, X), (0, Y), (0, DIAG), (first, 0), (first, Y), (first, DIAG)]
    targets_t, potential = paired(index, early_rows, late_rows, pieces, places, rows, feats)
    return (targets_t.T, potential[0])


def solution(mesh):
    in_specs = (P("batch", "group"), P("batch", "group"))
    out_specs = (P("batch", "group"), P())
    groups = mesh.shape["group"]
    paired_form = mesh.shape["batch"] == 4 and groups > 1 and groups & (groups - 1) == 0
    local = local_square if paired_form else local_any
    return jax.shard_map(local, mesh=mesh, in_specs=in_specs, out_specs=out_specs, check_vma=False)
```

```python
import functools
import math

import jax
import jax.numpy as jnp
from jax import lax
from jax.experimental import pallas as pl
from jax.experimental.pallas import tpu as pltpu
from jax.sharding import PartitionSpec as P

ITERS = 4
FEAT = 99840


def combined_all(value, axis, join):
    pieces = jax.tree.map(lambda part: lax.all_gather(part, axis), value)
    head = jax.tree.map(lambda part: part[0], pieces)
    tail = jax.tree.map(lambda part: part[1:], pieces)
    total, _ = lax.scan(lambda total, slab: (join(total, slab), None), head, tail)
    return total


def combine_parts(first, second):
    top = jnp.maximum(first[0], second[0])
    total = first[1] * jnp.exp(first[0] - top) + second[1] * jnp.exp(second[0] - top)
    return (top, total)


def local_parts(values, axis):
    top = jnp.max(values, axis=axis)
    total = jnp.sum(jnp.exp(values - jnp.expand_dims(top, axis)), axis=axis)
    return (top, total)


def local_any(noise, data):
    eps = 2.0 / jnp.sqrt(jnp.float32(FEAT))
    batch_total = noise.shape[0] * lax.axis_size("batch")
    loga = -jnp.log(jnp.float32(batch_total))
    noise_sq = jnp.sum(jnp.square(noise.astype(jnp.float32)), axis=1)
    all_rows = lax.all_gather(data, "batch", axis=0, tiled=True)
    piece_sq = jnp.sum(jnp.square(all_rows.astype(jnp.float32)), axis=1)
    cross = lax.dot_general(
        noise, all_rows, (((1,), (1,)), ((), ())), preferred_element_type=jnp.float32
    )
    partial_value = noise_sq[:, None] + piece_sq[None, :] - 2.0 * cross
    cost = lax.psum(partial_value, "group") / jnp.float32(FEAT)
    potential = jnp.zeros((batch_total,), jnp.float32)
    for step in range(ITERS):
        top, total = local_parts((potential[None, :] - cost) / eps, 1)
        rowpot = eps * loga - eps * (top + jnp.log(total))
        parts = local_parts((rowpot[:, None] - cost) / eps, 0)
        top, total = combined_all(parts, "batch", combine_parts)
        potential = eps * loga - eps * (top + jnp.log(total))
    scores = (potential[None, :] - cost) / eps
    top, total = local_parts(scores, 1)
    weights = jnp.exp(scores - (top + jnp.log(total))[:, None]).astype(jnp.bfloat16)
    targets = jnp.dot(weights, all_rows, preferred_element_type=jnp.float32)
    return (targets.astype(jnp.bfloat16), potential)


X, Y, DIAG = 1, 2, 3


def swap(value, way):
    return lax.ppermute(value, "batch", [(i, i ^ way) for i in range(4)])


VMEM = pl.BlockSpec(memory_space=pltpu.VMEM)
SMEM = pl.BlockSpec(memory_space=pltpu.SMEM)
HBM = pl.BlockSpec(memory_space=pltpu.HBM)


PARTS = 4


def cross_kernel(spans, noise_ref, *refs):
    *refs, out_ref = refs
    width = noise_ref.shape[0]
    for k, block_spans in enumerate(spans):
        (prior_ref, *pieces), refs = refs[: 1 + len(block_spans)], refs[1 + len(block_spans):]
        total = prior_ref[...]
        for (start, size), piece_ref in zip(block_spans, pieces):
            step = -(-size // (PARTS * 128)) * 128
            sums = []
            for at in range(0, size, step):
                deep = min(step, size - at)
                piece = piece_ref[at : at + deep, :]
                noise = noise_ref[:, start + at : start + at + deep]
                cross = jnp.dot(noise, piece, preferred_element_type=jnp.float32)
                square = jnp.sum(jnp.square(piece.astype(jnp.float32)), axis=0, keepdims=True)
                sums.append(square - 2.0 * cross)
            total = total + functools.reduce(lambda first, second: first + second, sums)
        out_ref[:, k * width : (k + 1) * width] = total


def crossed(noise, *blocks):
    rows = noise.shape[0]
    spans = [block[2::2] for block in blocks]
    values = [value for block in blocks for value in (block[0],) + block[1::2]]
    flops = sum(2 * rows * rows * size for block_spans in spans for _, size in block_spans)
    return pl.pallas_call(
        functools.partial(cross_kernel, spans),
        out_shape=jax.ShapeDtypeStruct((rows, rows * len(blocks)), jnp.float32),
        in_specs=[VMEM] * (1 + len(values)),
        out_specs=VMEM,
        compiler_params=pltpu.CompilerParams(vmem_limit_bytes=16 * 2**20),
        cost_estimate=pl.CostEstimate(flops=flops, bytes_accessed=flops // 64, transcendentals=0),
    )(noise, *values)


STEP = 64
TILES = 5


def pair_kernel(rows, feats, places, index_ref, *refs):
    early_refs, late_refs, refs = (refs[:4], refs[4:8]), refs[8:12], refs[12:]
    pieces, refs = refs[: len(places)], refs[len(places):]
    targets_ref, potential_ref, blocks, held, scores, out, in_sem, out_sem = refs
    batch = 4 * rows
    eps = 2.0 / FEAT**0.5
    ln2 = math.log(2.0)
    scale = -1.0 / (FEAT * eps * ln2)
    loga = -math.log2(batch)
    own, core = index_ref[0], index_ref[1]
    half = rows // 2

    loads = []
    for k, (start, r) in enumerate(places):
        copy = pltpu.make_async_copy(
            pieces[k],
            held.at[pl.ds(start, pieces[k].shape[0]), pl.ds(r * rows, rows)],
            in_sem.at[k],
        )
        copy.start()
        loads.append(copy)

    def block(i):
        return pl.ds(pl.multiple_of(i * rows, rows), rows)

    for p in range(4):
        for side in range(2):
            into = pl.ds(pl.multiple_of((own ^ p) * rows + (core ^ side) * half, half), half)
            for r in range(DIAG):
                blocks[into, block(own ^ (p ^ r))] = early_refs[side][p][:, block(r)] * scale
        blocks[block(own ^ p), block(own ^ (p ^ DIAG))] = late_refs[p][...].T * scale

    def sweep(_, v):
        u = []
        top = jnp.full((1, batch), -jnp.inf, jnp.float32)
        for c in range(batch // STEP):
            k = blocks[pl.ds(c * STEP, STEP), :]
            a = k + v
            m = jnp.max(a, axis=1, keepdims=True)
            s = jnp.sum(jnp.exp2(a - m), axis=1, keepdims=True)
            u.append(loga - (m + jnp.log2(s)))
            top = jnp.maximum(top, jnp.max(k + u[-1], axis=0, keepdims=True))
        total = jnp.zeros((1, batch), jnp.float32)
        for c in range(batch // STEP):
            a = blocks[pl.ds(c * STEP, STEP), :] + u[c]
            total = total + jnp.sum(jnp.exp2(a - top), axis=0, keepdims=True)
        return loga - (top + jnp.log2(total))

    v = lax.fori_loop(0, ITERS, sweep, jnp.zeros((1, batch), jnp.float32))
    potential_ref[...] = v * (eps * ln2)

    a = blocks[block(own), :] + v
    m = jnp.max(a, axis=1, keepdims=True)
    s = jnp.sum(jnp.exp2(a - m), axis=1, keepdims=True)
    scores[...] = jnp.exp2(a - (m + jnp.log2(s)))
    w = jnp.concatenate([scores[:, block(own ^ r)].T for r in range(4)], axis=0).astype(jnp.bfloat16)
    tile = feats // TILES

    def stored(t):
        part = pl.ds(pl.multiple_of(t * tile, 16), tile)
        return pltpu.make_async_copy(out.at[part, :], targets_ref.at[part, :], out_sem.at[t])

    def multiply(t, _):
        part = pl.ds(pl.multiple_of(t * tile, 16), tile)
        out[part, :] = jnp.dot(held[part, :], w, preferred_element_type=jnp.float32).astype(jnp.bfloat16)
        stored(t).start()
        return 0

    later = max(start for start, _ in places)
    for copy, (start, _) in zip(loads, places):
        if start < later:
            copy.wait()
    lax.fori_loop(0, later // tile, multiply, 0)
    for copy, (start, _) in zip(loads, places):
        if start >= later:
            copy.wait()
    lax.fori_loop(later // tile, TILES, multiply, 0)
    for t in range(TILES):
        stored(t).wait()


def paired(index, early, late, pieces, places, rows, feats):
    batch = 4 * rows
    return pl.pallas_call(
        functools.partial(pair_kernel, rows, feats, places),
        out_shape=(
            jax.ShapeDtypeStruct((feats, rows), jnp.bfloat16),
            jax.ShapeDtypeStruct((1, batch), jnp.float32),
        ),
        in_specs=[SMEM] + [VMEM] * 12 + [HBM] * len(pieces),
        out_specs=(HBM, VMEM),
        scratch_shapes=[
            pltpu.VMEM((batch, batch), jnp.float32),
            pltpu.VMEM((feats, batch), jnp.bfloat16),
            pltpu.VMEM((rows, batch), jnp.float32),
            pltpu.VMEM((feats, rows), jnp.bfloat16),
            pltpu.SemaphoreType.DMA((len(pieces),)),
            pltpu.SemaphoreType.DMA((TILES,)),
        ],
        compiler_params=pltpu.CompilerParams(vmem_limit_bytes=24 * 2**20),
        cost_estimate=pl.CostEstimate(
            flops=2 * rows * batch * feats, bytes_accessed=10 * rows * feats, transcendentals=9 * batch * batch
        ),
    )(index, *early, *late, *pieces)


def squared(values_t):
    return jnp.sum(jnp.square(values_t.astype(jnp.float32)), axis=0)


def turn(value, way):
    groups = lax.axis_size("group")
    return lax.ppermute(value, "group", [(g, g ^ way) for g in range(groups)])


def group_share(value):
    groups = lax.axis_size("group")
    rows, width = value.shape
    share = rows // groups
    parts = value.reshape(2, groups // 2, share, width).transpose(1, 0, 2, 3).reshape(rows, width)
    parts = lax.all_to_all(parts, "group", 0, 0, tiled=True)
    return jnp.sum(parts.reshape(groups, share, width), axis=0)


def line_gather(value, place):
    lines = lax.axis_size("group") // 2
    shares = jnp.stack([value] + [turn(value, 2 * way) for way in range(1, lines)])
    return jnp.concatenate(
        [lax.dynamic_index_in_dim(shares, place ^ jnp.uint32(z), keepdims=False) for z in range(lines)]
    )


def product(first_t, second_t):
    return lax.dot_general(
        first_t, second_t, (((0,), (0,)), ((), ())), preferred_element_type=jnp.float32
    )


def batch_swaps(value):
    return [value, swap(value, X), swap(value, Y), swap(value, DIAG)]


def local_square(noise, data):
    rows, feats = noise.shape
    noise_t, data_t = noise.T, data.T
    own, group = lax.axis_index("batch"), lax.axis_index("group").astype(jnp.uint32)
    core, line = group & 1, group >> 1
    index = jnp.stack([own.astype(jnp.int32), core.astype(jnp.int32)])

    first = feats * 8 // (15 * 128) * 128
    low, high = (0, first), (first, feats - first)
    d_low, d_high = data_t[:first], data_t[first:]
    x_all, y_low, y_high = swap(data_t, X), swap(d_low, Y), swap(d_high, Y)
    noise_sq, data_sq = squared(noise_t), squared(data_t)
    diag_sq = swap(data_sq, DIAG)
    n_low, n_high = noise_t[:first], noise_t[first:]
    start = jnp.broadcast_to(noise_sq[:, None], (rows, rows))
    own_cost = crossed(noise, (start, d_low, low, d_high, high))
    y_cost = crossed(noise, (start, y_low, low))
    y_low, own_cost, y_cost, data_sq, n_low, n_high = lax.optimization_barrier(
        (y_low, own_cost, y_cost, data_sq, n_low, n_high)
    )
    diag_low = swap(y_low, X)
    x_tail = x_all[first:]
    diag_high = swap(x_tail, Y)
    x_all, y_high, x_tail = lax.optimization_barrier((x_all, y_high, x_tail))
    early = crossed(noise, (own_cost,), (start, x_all, (0, feats)), (y_cost, y_high, high))
    early_half = line_gather(group_share(early), line)
    early_mine = batch_swaps(early_half)
    _, diag_high, diag_sq = lax.optimization_barrier((early_half, diag_high, diag_sq))
    _, diag_low = lax.optimization_barrier((early_half, diag_low))
    late = noise_sq[None, :] + diag_sq[:, None] - 2.0 * (product(diag_high, n_high) + product(diag_low, n_low))
    late, *early_mine = lax.optimization_barrier((late, *early_mine))
    early_rows = early_mine + [turn(value, 1) for value in early_mine]
    late = late + turn(late, 1)
    late, *early_rows = lax.optimization_barrier((late, *early_rows))
    way = 2
    while way < lax.axis_size("group"):
        late = late + turn(late, way)
        way *= 2
    late_rows = batch_swaps(late)

    pieces = [d_low, x_all, y_low, diag_low, d_high, y_high, diag_high]
    places = [(0, 0), (0, X), (0, Y), (0, DIAG), (first, 0), (first, Y), (first, DIAG)]
    targets_t, potential = paired(index, early_rows, late_rows, pieces, places, rows, feats)
    return (targets_t.T, potential[0])


def solution(mesh):
    in_specs = (P("batch", "group"), P("batch", "group"))
    out_specs = (P("batch", "group"), P())
    groups = mesh.shape["group"]
    paired_form = mesh.shape["batch"] == 4 and groups > 1 and groups & (groups - 1) == 0
    local = local_square if paired_form else local_any
    return jax.shard_map(local, mesh=mesh, in_specs=in_specs, out_specs=out_specs, check_vma=False)
```

```python
import functools
import math

import jax
import jax.numpy as jnp
from jax import lax
from jax.experimental import pallas as pl
from jax.experimental.pallas import tpu as pltpu
from jax.sharding import PartitionSpec as P

ITERS = 4
FEAT = 99840


def combined_all(value, axis, join):
    pieces = jax.tree.map(lambda part: lax.all_gather(part, axis), value)
    head = jax.tree.map(lambda part: part[0], pieces)
    tail = jax.tree.map(lambda part: part[1:], pieces)
    total, _ = lax.scan(lambda total, slab: (join(total, slab), None), head, tail)
    return total


def combine_parts(first, second):
    top = jnp.maximum(first[0], second[0])
    total = first[1] * jnp.exp(first[0] - top) + second[1] * jnp.exp(second[0] - top)
    return (top, total)


def local_parts(values, axis):
    top = jnp.max(values, axis=axis)
    total = jnp.sum(jnp.exp(values - jnp.expand_dims(top, axis)), axis=axis)
    return (top, total)


def local_any(noise, data):
    eps = 2.0 / jnp.sqrt(jnp.float32(FEAT))
    batch_total = noise.shape[0] * lax.axis_size("batch")
    loga = -jnp.log(jnp.float32(batch_total))
    noise_sq = jnp.sum(jnp.square(noise.astype(jnp.float32)), axis=1)
    all_rows = lax.all_gather(data, "batch", axis=0, tiled=True)
    piece_sq = jnp.sum(jnp.square(all_rows.astype(jnp.float32)), axis=1)
    cross = lax.dot_general(
        noise, all_rows, (((1,), (1,)), ((), ())), preferred_element_type=jnp.float32
    )
    partial_value = noise_sq[:, None] + piece_sq[None, :] - 2.0 * cross
    cost = lax.psum(partial_value, "group") / jnp.float32(FEAT)
    potential = jnp.zeros((batch_total,), jnp.float32)
    for step in range(ITERS):
        top, total = local_parts((potential[None, :] - cost) / eps, 1)
        rowpot = eps * loga - eps * (top + jnp.log(total))
        parts = local_parts((rowpot[:, None] - cost) / eps, 0)
        top, total = combined_all(parts, "batch", combine_parts)
        potential = eps * loga - eps * (top + jnp.log(total))
    scores = (potential[None, :] - cost) / eps
    top, total = local_parts(scores, 1)
    weights = jnp.exp(scores - (top + jnp.log(total))[:, None]).astype(jnp.bfloat16)
    targets = jnp.dot(weights, all_rows, preferred_element_type=jnp.float32)
    return (targets.astype(jnp.bfloat16), potential)


X, Y, DIAG = 1, 2, 3


def swap(value, way):
    return lax.ppermute(value, "batch", [(i, i ^ way) for i in range(4)])


VMEM = pl.BlockSpec(memory_space=pltpu.VMEM)
SMEM = pl.BlockSpec(memory_space=pltpu.SMEM)
HBM = pl.BlockSpec(memory_space=pltpu.HBM)


PARTS = 4


def cross_kernel(spans, noise_ref, *refs):
    *refs, out_ref = refs
    width = noise_ref.shape[0]
    for k, block_spans in enumerate(spans):
        (prior_ref, *pieces), refs = refs[: 1 + len(block_spans)], refs[1 + len(block_spans):]
        total = prior_ref[...]
        for (start, size), piece_ref in zip(block_spans, pieces):
            step = -(-size // (PARTS * 128)) * 128
            sums = []
            for at in range(0, size, step):
                deep = min(step, size - at)
                piece = piece_ref[at : at + deep, :]
                noise = noise_ref[:, start + at : start + at + deep]
                cross = jnp.dot(noise, piece, preferred_element_type=jnp.float32)
                square = jnp.sum(jnp.square(piece.astype(jnp.float32)), axis=0, keepdims=True)
                sums.append(square - 2.0 * cross)
            total = total + functools.reduce(lambda first, second: first + second, sums)
        out_ref[:, k * width : (k + 1) * width] = total


def crossed(noise, *blocks):
    rows = noise.shape[0]
    spans = [block[2::2] for block in blocks]
    values = [value for block in blocks for value in (block[0],) + block[1::2]]
    flops = sum(2 * rows * rows * size for block_spans in spans for _, size in block_spans)
    return pl.pallas_call(
        functools.partial(cross_kernel, spans),
        out_shape=jax.ShapeDtypeStruct((rows, rows * len(blocks)), jnp.float32),
        in_specs=[VMEM] * (1 + len(values)),
        out_specs=VMEM,
        compiler_params=pltpu.CompilerParams(vmem_limit_bytes=16 * 2**20),
        cost_estimate=pl.CostEstimate(flops=flops, bytes_accessed=flops // 64, transcendentals=0),
    )(noise, *values)


STEP = 64
TILES = 5


def pair_kernel(rows, feats, places, index_ref, *refs):
    early_refs, late_refs, refs = (refs[:4], refs[4:8]), refs[8:10], refs[10:]
    pieces, refs = refs[: len(places)], refs[len(places):]
    targets_ref, potential_ref, blocks, held, scores, out, in_sem, out_sem = refs
    batch = 4 * rows
    eps = 2.0 / FEAT**0.5
    ln2 = math.log(2.0)
    scale = -1.0 / (FEAT * eps * ln2)
    loga = -math.log2(batch)
    own, core = index_ref[0], index_ref[1]
    half = rows // 2

    loads = []
    for k, (start, r) in enumerate(places):
        copy = pltpu.make_async_copy(
            pieces[k],
            held.at[pl.ds(start, pieces[k].shape[0]), pl.ds(r * rows, rows)],
            in_sem.at[k],
        )
        copy.start()
        loads.append(copy)

    def block(i):
        return pl.ds(pl.multiple_of(i * rows, rows), rows)

    for p in range(4):
        for side in range(2):
            part = pl.ds(p * half, half)
            into = pl.ds(pl.multiple_of((own ^ p) * rows + (core ^ side) * half, half), half)
            for r in range(DIAG):
                blocks[into, block(own ^ (p ^ r))] = early_refs[side][p][:, block(r)] * scale
            blocks[into, block(own ^ (p ^ DIAG))] = late_refs[side][part, :] * scale

    def sweep(_, v):
        u = []
        top = jnp.full((1, batch), -jnp.inf, jnp.float32)
        for c in range(batch // STEP):
            k = blocks[pl.ds(c * STEP, STEP), :]
            a = k + v
            m = jnp.max(a, axis=1, keepdims=True)
            s = jnp.sum(jnp.exp2(a - m), axis=1, keepdims=True)
            u.append(loga - (m + jnp.log2(s)))
            top = jnp.maximum(top, jnp.max(k + u[-1], axis=0, keepdims=True))
        total = jnp.zeros((1, batch), jnp.float32)
        for c in range(batch // STEP):
            a = blocks[pl.ds(c * STEP, STEP), :] + u[c]
            total = total + jnp.sum(jnp.exp2(a - top), axis=0, keepdims=True)
        return loga - (top + jnp.log2(total))

    v = lax.fori_loop(0, ITERS, sweep, jnp.zeros((1, batch), jnp.float32))
    potential_ref[...] = v * (eps * ln2)

    a = blocks[block(own), :] + v
    m = jnp.max(a, axis=1, keepdims=True)
    s = jnp.sum(jnp.exp2(a - m), axis=1, keepdims=True)
    scores[...] = jnp.exp2(a - (m + jnp.log2(s)))
    w = jnp.concatenate([scores[:, block(own ^ r)].T for r in range(4)], axis=0).astype(jnp.bfloat16)
    tile = feats // TILES

    def stored(t):
        part = pl.ds(pl.multiple_of(t * tile, 16), tile)
        return pltpu.make_async_copy(out.at[part, :], targets_ref.at[part, :], out_sem.at[t])

    def multiply(t, _):
        part = pl.ds(pl.multiple_of(t * tile, 16), tile)
        out[part, :] = jnp.dot(held[part, :], w, preferred_element_type=jnp.float32).astype(jnp.bfloat16)
        stored(t).start()
        return 0

    later = max(start for start, _ in places)
    for copy, (start, _) in zip(loads, places):
        if start < later:
            copy.wait()
    lax.fori_loop(0, later // tile, multiply, 0)
    for copy, (start, _) in zip(loads, places):
        if start >= later:
            copy.wait()
    lax.fori_loop(later // tile, TILES, multiply, 0)
    for t in range(TILES):
        stored(t).wait()


def paired(index, early, late, pieces, places, rows, feats):
    batch = 4 * rows
    return pl.pallas_call(
        functools.partial(pair_kernel, rows, feats, places),
        out_shape=(
            jax.ShapeDtypeStruct((feats, rows), jnp.bfloat16),
            jax.ShapeDtypeStruct((1, batch), jnp.float32),
        ),
        in_specs=[SMEM] + [VMEM] * 10 + [HBM] * len(pieces),
        out_specs=(HBM, VMEM),
        scratch_shapes=[
            pltpu.VMEM((batch, batch), jnp.float32),
            pltpu.VMEM((feats, batch), jnp.bfloat16),
            pltpu.VMEM((rows, batch), jnp.float32),
            pltpu.VMEM((feats, rows), jnp.bfloat16),
            pltpu.SemaphoreType.DMA((len(pieces),)),
            pltpu.SemaphoreType.DMA((TILES,)),
        ],
        compiler_params=pltpu.CompilerParams(vmem_limit_bytes=24 * 2**20),
        cost_estimate=pl.CostEstimate(
            flops=2 * rows * batch * feats, bytes_accessed=10 * rows * feats, transcendentals=9 * batch * batch
        ),
    )(index, *early, *late, *pieces)


def squared(values_t):
    return jnp.sum(jnp.square(values_t.astype(jnp.float32)), axis=0)


def turn(value, way):
    groups = lax.axis_size("group")
    return lax.ppermute(value, "group", [(g, g ^ way) for g in range(groups)])


def core_share(value, core):
    half = value.shape[0] // 2
    kept = lax.dynamic_slice_in_dim(value, core * jnp.uint32(half), half)
    given = lax.dynamic_slice_in_dim(value, (1 - core) * jnp.uint32(half), half)
    return kept + turn(given, 1)


def line_sum(value):
    way = 2
    while way < lax.axis_size("group"):
        value = value + turn(value, way)
        way *= 2
    return value


def group_share(value):
    groups = lax.axis_size("group")
    rows, width = value.shape
    share = rows // groups
    parts = value.reshape(2, groups // 2, share, width).transpose(1, 0, 2, 3).reshape(rows, width)
    parts = lax.all_to_all(parts, "group", 0, 0, tiled=True)
    return jnp.sum(parts.reshape(groups, share, width), axis=0)


def line_gather(value, place):
    lines = lax.axis_size("group") // 2
    shares = jnp.stack([value] + [turn(value, 2 * way) for way in range(1, lines)])
    return jnp.concatenate(
        [lax.dynamic_index_in_dim(shares, place ^ jnp.uint32(z), keepdims=False) for z in range(lines)]
    )


def batch_swaps(value):
    return [value, swap(value, X), swap(value, Y), swap(value, DIAG)]


def local_square(noise, data):
    rows, feats = noise.shape
    noise_t, data_t = noise.T, data.T
    own, group = lax.axis_index("batch"), lax.axis_index("group").astype(jnp.uint32)
    core, line = group & 1, group >> 1
    index = jnp.stack([own.astype(jnp.int32), core.astype(jnp.int32)])

    first = feats * 8 // (15 * 128) * 128
    low, high = (0, first), (first, feats - first)
    d_low, d_high = data_t[:first], data_t[first:]
    x_all, y_low, y_high = swap(data_t, X), swap(d_low, Y), swap(d_high, Y)
    start = jnp.broadcast_to(squared(noise_t)[:, None], (rows, rows))
    own_cost = crossed(noise, (start, d_low, low, d_high, high))
    y_cost = crossed(noise, (start, y_low, low))
    y_low, own_cost, y_cost = lax.optimization_barrier((y_low, own_cost, y_cost))
    diag_low = swap(y_low, X)
    x_tail = x_all[first:]
    diag_high = swap(x_tail, Y)
    x_all, y_high, x_tail = lax.optimization_barrier((x_all, y_high, x_tail))
    early = crossed(noise, (own_cost,), (start, x_all, (0, feats)), (y_cost, y_high, high))
    early_half = line_gather(group_share(early), line)
    early_mine = batch_swaps(early_half)
    _, diag_low = lax.optimization_barrier((early_half, diag_low))
    late = crossed(noise, (start, diag_low, low))
    _, diag_high = lax.optimization_barrier((early_half, diag_high))
    late = crossed(noise, (late, diag_high, high))
    late, *early_mine = lax.optimization_barrier((late, *early_mine))
    early_rows = early_mine + [turn(value, 1) for value in early_mine]
    late_half = core_share(late, core)
    late_half, *early_rows = lax.optimization_barrier((late_half, *early_rows))
    late_half = line_sum(late_half)
    late_mine = jnp.concatenate(batch_swaps(late_half))
    late_rows = [late_mine, turn(late_mine, 1)]

    pieces = [d_low, x_all, y_low, diag_low, d_high, y_high, diag_high]
    places = [(0, 0), (0, X), (0, Y), (0, DIAG), (first, 0), (first, Y), (first, DIAG)]
    targets_t, potential = paired(index, early_rows, late_rows, pieces, places, rows, feats)
    return (targets_t.T, potential[0])


def solution(mesh):
    in_specs = (P("batch", "group"), P("batch", "group"))
    out_specs = (P("batch", "group"), P())
    groups = mesh.shape["group"]
    paired_form = mesh.shape["batch"] == 4 and groups > 1 and groups & (groups - 1) == 0
    local = local_square if paired_form else local_any
    return jax.shard_map(local, mesh=mesh, in_specs=in_specs, out_specs=out_specs, check_vma=False)
```

```python
import functools
import math

import jax
import jax.numpy as jnp
from jax import lax
from jax.experimental import pallas as pl
from jax.experimental.pallas import tpu as pltpu
from jax.sharding import PartitionSpec as P

ITERS = 4
FEAT = 99840


def combined_all(value, axis, join):
    pieces = jax.tree.map(lambda part: lax.all_gather(part, axis), value)
    head = jax.tree.map(lambda part: part[0], pieces)
    tail = jax.tree.map(lambda part: part[1:], pieces)
    total, _ = lax.scan(lambda total, slab: (join(total, slab), None), head, tail)
    return total


def combine_parts(first, second):
    top = jnp.maximum(first[0], second[0])
    total = first[1] * jnp.exp(first[0] - top) + second[1] * jnp.exp(second[0] - top)
    return (top, total)


def local_parts(values, axis):
    top = jnp.max(values, axis=axis)
    total = jnp.sum(jnp.exp(values - jnp.expand_dims(top, axis)), axis=axis)
    return (top, total)


def local_any(noise, data):
    eps = 2.0 / jnp.sqrt(jnp.float32(FEAT))
    batch_total = noise.shape[0] * lax.axis_size("batch")
    loga = -jnp.log(jnp.float32(batch_total))
    noise_sq = jnp.sum(jnp.square(noise.astype(jnp.float32)), axis=1)
    all_rows = lax.all_gather(data, "batch", axis=0, tiled=True)
    piece_sq = jnp.sum(jnp.square(all_rows.astype(jnp.float32)), axis=1)
    cross = lax.dot_general(
        noise, all_rows, (((1,), (1,)), ((), ())), preferred_element_type=jnp.float32
    )
    partial_value = noise_sq[:, None] + piece_sq[None, :] - 2.0 * cross
    cost = lax.psum(partial_value, "group") / jnp.float32(FEAT)
    potential = jnp.zeros((batch_total,), jnp.float32)
    for step in range(ITERS):
        top, total = local_parts((potential[None, :] - cost) / eps, 1)
        rowpot = eps * loga - eps * (top + jnp.log(total))
        parts = local_parts((rowpot[:, None] - cost) / eps, 0)
        top, total = combined_all(parts, "batch", combine_parts)
        potential = eps * loga - eps * (top + jnp.log(total))
    scores = (potential[None, :] - cost) / eps
    top, total = local_parts(scores, 1)
    weights = jnp.exp(scores - (top + jnp.log(total))[:, None]).astype(jnp.bfloat16)
    targets = jnp.dot(weights, all_rows, preferred_element_type=jnp.float32)
    return (targets.astype(jnp.bfloat16), potential)


X, Y, DIAG = 1, 2, 3


def swap(value, way):
    return lax.ppermute(value, "batch", [(i, i ^ way) for i in range(4)])


VMEM = pl.BlockSpec(memory_space=pltpu.VMEM)
SMEM = pl.BlockSpec(memory_space=pltpu.SMEM)
HBM = pl.BlockSpec(memory_space=pltpu.HBM)


PARTS = 4


def cross_kernel(spans, noise_ref, *refs):
    *refs, out_ref = refs
    width = noise_ref.shape[0]
    for k, block_spans in enumerate(spans):
        (prior_ref, *pieces), refs = refs[: 1 + len(block_spans)], refs[1 + len(block_spans):]
        total = prior_ref[...]
        for (start, size), piece_ref in zip(block_spans, pieces):
            step = -(-size // (PARTS * 128)) * 128
            sums = []
            for at in range(0, size, step):
                deep = min(step, size - at)
                piece = piece_ref[at : at + deep, :]
                noise = noise_ref[:, start + at : start + at + deep]
                cross = jnp.dot(noise, piece, preferred_element_type=jnp.float32)
                square = jnp.sum(jnp.square(piece.astype(jnp.float32)), axis=0, keepdims=True)
                sums.append(square - 2.0 * cross)
            total = total + functools.reduce(lambda first, second: first + second, sums)
        out_ref[:, k * width : (k + 1) * width] = total


def crossed(noise, *blocks):
    rows = noise.shape[0]
    spans = [block[2::2] for block in blocks]
    values = [value for block in blocks for value in (block[0],) + block[1::2]]
    flops = sum(2 * rows * rows * size for block_spans in spans for _, size in block_spans)
    return pl.pallas_call(
        functools.partial(cross_kernel, spans),
        out_shape=jax.ShapeDtypeStruct((rows, rows * len(blocks)), jnp.float32),
        in_specs=[VMEM] * (1 + len(values)),
        out_specs=VMEM,
        compiler_params=pltpu.CompilerParams(vmem_limit_bytes=16 * 2**20),
        cost_estimate=pl.CostEstimate(flops=flops, bytes_accessed=flops // 64, transcendentals=0),
    )(noise, *values)


STEP = 64
TILES = 5


def pair_kernel(rows, feats, places, index_ref, *refs):
    early_refs, late_ref, refs = (refs[:4], refs[4:8]), refs[8], refs[9:]
    pieces, refs = refs[: len(places)], refs[len(places):]
    targets_ref, potential_ref, blocks, held, scores, out, in_sem, out_sem = refs
    batch = 4 * rows
    eps = 2.0 / FEAT**0.5
    ln2 = math.log(2.0)
    scale = -1.0 / (FEAT * eps * ln2)
    loga = -math.log2(batch)
    own, core = index_ref[0], index_ref[1]
    half = rows // 2

    loads = []
    for k, (start, r) in enumerate(places):
        copy = pltpu.make_async_copy(
            pieces[k],
            held.at[pl.ds(start, pieces[k].shape[0]), pl.ds(r * rows, rows)],
            in_sem.at[k],
        )
        copy.start()
        loads.append(copy)

    def block(i):
        return pl.ds(pl.multiple_of(i * rows, rows), rows)

    for p in range(4):
        for side in range(2):
            into = pl.ds(pl.multiple_of((own ^ p) * rows + (core ^ side) * half, half), half)
            for r in range(DIAG):
                blocks[into, block(own ^ (p ^ r))] = early_refs[side][p][:, block(r)] * scale
        blocks[block(own ^ p), block(own ^ (p ^ DIAG))] = late_ref[block(p), :] * scale

    def sweep(_, v):
        u = []
        top = jnp.full((1, batch), -jnp.inf, jnp.float32)
        for c in range(batch // STEP):
            k = blocks[pl.ds(c * STEP, STEP), :]
            a = k + v
            m = jnp.max(a, axis=1, keepdims=True)
            s = jnp.sum(jnp.exp2(a - m), axis=1, keepdims=True)
            u.append(loga - (m + jnp.log2(s)))
            top = jnp.maximum(top, jnp.max(k + u[-1], axis=0, keepdims=True))
        total = jnp.zeros((1, batch), jnp.float32)
        for c in range(batch // STEP):
            a = blocks[pl.ds(c * STEP, STEP), :] + u[c]
            total = total + jnp.sum(jnp.exp2(a - top), axis=0, keepdims=True)
        return loga - (top + jnp.log2(total))

    v = lax.fori_loop(0, ITERS, sweep, jnp.zeros((1, batch), jnp.float32))
    potential_ref[...] = v * (eps * ln2)

    a = blocks[block(own), :] + v
    m = jnp.max(a, axis=1, keepdims=True)
    s = jnp.sum(jnp.exp2(a - m), axis=1, keepdims=True)
    scores[...] = jnp.exp2(a - (m + jnp.log2(s)))
    w = jnp.concatenate([scores[:, block(own ^ r)].T for r in range(4)], axis=0).astype(jnp.bfloat16)
    tile = feats // TILES

    def stored(t):
        part = pl.ds(pl.multiple_of(t * tile, 16), tile)
        return pltpu.make_async_copy(out.at[part, :], targets_ref.at[part, :], out_sem.at[t])

    def multiply(t, _):
        part = pl.ds(pl.multiple_of(t * tile, 16), tile)
        out[part, :] = jnp.dot(held[part, :], w, preferred_element_type=jnp.float32).astype(jnp.bfloat16)
        stored(t).start()
        return 0

    later = max(start for start, _ in places)
    for copy, (start, _) in zip(loads, places):
        if start < later:
            copy.wait()
    lax.fori_loop(0, later // tile, multiply, 0)
    for copy, (start, _) in zip(loads, places):
        if start >= later:
            copy.wait()
    lax.fori_loop(later // tile, TILES, multiply, 0)
    for t in range(TILES):
        stored(t).wait()


def paired(index, early, late, pieces, places, rows, feats):
    batch = 4 * rows
    return pl.pallas_call(
        functools.partial(pair_kernel, rows, feats, places),
        out_shape=(
            jax.ShapeDtypeStruct((feats, rows), jnp.bfloat16),
            jax.ShapeDtypeStruct((1, batch), jnp.float32),
        ),
        in_specs=[SMEM] + [VMEM] * 9 + [HBM] * len(pieces),
        out_specs=(HBM, VMEM),
        scratch_shapes=[
            pltpu.VMEM((batch, batch), jnp.float32),
            pltpu.VMEM((feats, batch), jnp.bfloat16),
            pltpu.VMEM((rows, batch), jnp.float32),
            pltpu.VMEM((feats, rows), jnp.bfloat16),
            pltpu.SemaphoreType.DMA((len(pieces),)),
            pltpu.SemaphoreType.DMA((TILES,)),
        ],
        compiler_params=pltpu.CompilerParams(vmem_limit_bytes=20 * 2**20),
        cost_estimate=pl.CostEstimate(
            flops=2 * rows * batch * feats, bytes_accessed=10 * rows * feats, transcendentals=9 * batch * batch
        ),
    )(index, *early, *late, *pieces)


def squared(values_t):
    return jnp.sum(jnp.square(values_t.astype(jnp.float32)), axis=0)


def turn(value, way):
    groups = lax.axis_size("group")
    return lax.ppermute(value, "group", [(g, g ^ way) for g in range(groups)])


def group_share(value):
    groups = lax.axis_size("group")
    rows, width = value.shape
    share = rows // groups
    parts = value.reshape(2, groups // 2, share, width).transpose(1, 0, 2, 3).reshape(rows, width)
    parts = lax.all_to_all(parts, "group", 0, 0, tiled=True)
    return jnp.sum(parts.reshape(groups, share, width), axis=0)


def line_gather(value, place):
    lines = lax.axis_size("group") // 2
    shares = jnp.stack([value] + [turn(value, 2 * way) for way in range(1, lines)])
    return jnp.concatenate(
        [lax.dynamic_index_in_dim(shares, place ^ jnp.uint32(z), keepdims=False) for z in range(lines)]
    )


def batch_swaps(value):
    return [value, swap(value, X), swap(value, Y), swap(value, DIAG)]


def local_square(noise, data):
    rows, feats = noise.shape
    noise_t, data_t = noise.T, data.T
    own, group = lax.axis_index("batch"), lax.axis_index("group").astype(jnp.uint32)
    core, line = group & 1, group >> 1
    index = jnp.stack([own.astype(jnp.int32), core.astype(jnp.int32)])

    first = feats * 8 // (15 * 128) * 128
    low, high = (0, first), (first, feats - first)
    d_low, d_high = data_t[:first], data_t[first:]
    x_all, y_low, y_high = swap(data_t, X), swap(d_low, Y), swap(d_high, Y)
    start = jnp.broadcast_to(squared(noise_t)[:, None], (rows, rows))
    own_cost = crossed(noise, (start, d_low, low, d_high, high))
    y_cost = crossed(noise, (start, y_low, low))
    y_low, own_cost, y_cost = lax.optimization_barrier((y_low, own_cost, y_cost))
    diag_low = swap(y_low, X)
    x_tail = x_all[first:]
    diag_high = swap(x_tail, Y)
    x_all, y_high, x_tail = lax.optimization_barrier((x_all, y_high, x_tail))
    early = crossed(noise, (own_cost,), (start, x_all, (0, feats)), (y_cost, y_high, high))
    early_half = line_gather(group_share(early), line)
    early_mine = batch_swaps(early_half)
    _, diag_low = lax.optimization_barrier((early_half, diag_low))
    late = crossed(noise, (start, diag_low, low))
    _, diag_high = lax.optimization_barrier((early_half, diag_high))
    late = crossed(noise, (late, diag_high, high))
    late, *early_mine = lax.optimization_barrier((late, *early_mine))
    early_rows = early_mine + [turn(value, 1) for value in early_mine]
    way = 1
    while way < lax.axis_size("group"):
        late = late + turn(late, way)
        if way == 2:
            late, *early_rows = lax.optimization_barrier((late, *early_rows))
        way *= 2
    late_rows = [jnp.concatenate(batch_swaps(late))]

    pieces = [d_low, x_all, y_low, diag_low, d_high, y_high, diag_high]
    places = [(0, 0), (0, X), (0, Y), (0, DIAG), (first, 0), (first, Y), (first, DIAG)]
    targets_t, potential = paired(index, early_rows, late_rows, pieces, places, rows, feats)
    return (targets_t.T, potential[0])


def solution(mesh):
    in_specs = (P("batch", "group"), P("batch", "group"))
    out_specs = (P("batch", "group"), P())
    groups = mesh.shape["group"]
    paired_form = mesh.shape["batch"] == 4 and groups > 1 and groups & (groups - 1) == 0
    local = local_square if paired_form else local_any
    return jax.shard_map(local, mesh=mesh, in_specs=in_specs, out_specs=out_specs, check_vma=False)
```

```python
import functools
import math

import jax
import jax.numpy as jnp
from jax import lax
from jax.experimental import pallas as pl
from jax.experimental.pallas import tpu as pltpu
from jax.sharding import PartitionSpec as P

ITERS = 4
FEAT = 99840


def combined_all(value, axis, join):
    pieces = jax.tree.map(lambda part: lax.all_gather(part, axis), value)
    head = jax.tree.map(lambda part: part[0], pieces)
    tail = jax.tree.map(lambda part: part[1:], pieces)
    total, _ = lax.scan(lambda total, slab: (join(total, slab), None), head, tail)
    return total


def combine_parts(first, second):
    top = jnp.maximum(first[0], second[0])
    total = first[1] * jnp.exp(first[0] - top) + second[1] * jnp.exp(second[0] - top)
    return (top, total)


def local_parts(values, axis):
    top = jnp.max(values, axis=axis)
    total = jnp.sum(jnp.exp(values - jnp.expand_dims(top, axis)), axis=axis)
    return (top, total)


def local_any(noise, data):
    eps = 2.0 / jnp.sqrt(jnp.float32(FEAT))
    batch_total = noise.shape[0] * lax.axis_size("batch")
    loga = -jnp.log(jnp.float32(batch_total))
    noise_sq = jnp.sum(jnp.square(noise.astype(jnp.float32)), axis=1)
    all_rows = lax.all_gather(data, "batch", axis=0, tiled=True)
    piece_sq = jnp.sum(jnp.square(all_rows.astype(jnp.float32)), axis=1)
    cross = lax.dot_general(
        noise, all_rows, (((1,), (1,)), ((), ())), preferred_element_type=jnp.float32
    )
    partial_value = noise_sq[:, None] + piece_sq[None, :] - 2.0 * cross
    cost = lax.psum(partial_value, "group") / jnp.float32(FEAT)
    potential = jnp.zeros((batch_total,), jnp.float32)
    for step in range(ITERS):
        top, total = local_parts((potential[None, :] - cost) / eps, 1)
        rowpot = eps * loga - eps * (top + jnp.log(total))
        parts = local_parts((rowpot[:, None] - cost) / eps, 0)
        top, total = combined_all(parts, "batch", combine_parts)
        potential = eps * loga - eps * (top + jnp.log(total))
    scores = (potential[None, :] - cost) / eps
    top, total = local_parts(scores, 1)
    weights = jnp.exp(scores - (top + jnp.log(total))[:, None]).astype(jnp.bfloat16)
    targets = jnp.dot(weights, all_rows, preferred_element_type=jnp.float32)
    return (targets.astype(jnp.bfloat16), potential)


X, Y, DIAG = 1, 2, 3


def swap(value, way):
    return lax.ppermute(value, "batch", [(i, i ^ way) for i in range(4)])


VMEM = pl.BlockSpec(memory_space=pltpu.VMEM)
SMEM = pl.BlockSpec(memory_space=pltpu.SMEM)
HBM = pl.BlockSpec(memory_space=pltpu.HBM)


PARTS = 4


def cross_kernel(spans, noise_ref, *refs):
    *refs, out_ref = refs
    width = noise_ref.shape[0]
    for k, block_spans in enumerate(spans):
        (prior_ref, *pieces), refs = refs[: 1 + len(block_spans)], refs[1 + len(block_spans):]
        total = prior_ref[...]
        for (start, size), piece_ref in zip(block_spans, pieces):
            step = -(-size // (PARTS * 128)) * 128
            sums = []
            for at in range(0, size, step):
                deep = min(step, size - at)
                piece = piece_ref[at : at + deep, :]
                noise = noise_ref[:, start + at : start + at + deep]
                cross = jnp.dot(noise, piece, preferred_element_type=jnp.float32)
                square = jnp.sum(jnp.square(piece.astype(jnp.float32)), axis=0, keepdims=True)
                sums.append(square - 2.0 * cross)
            total = total + functools.reduce(lambda first, second: first + second, sums)
        out_ref[:, k * width : (k + 1) * width] = total


def crossed(noise, *blocks):
    rows = noise.shape[0]
    spans = [block[2::2] for block in blocks]
    values = [value for block in blocks for value in (block[0],) + block[1::2]]
    flops = sum(2 * rows * rows * size for block_spans in spans for _, size in block_spans)
    return pl.pallas_call(
        functools.partial(cross_kernel, spans),
        out_shape=jax.ShapeDtypeStruct((rows, rows * len(blocks)), jnp.float32),
        in_specs=[VMEM] * (1 + len(values)),
        out_specs=VMEM,
        compiler_params=pltpu.CompilerParams(vmem_limit_bytes=12 * 2**20),
        cost_estimate=pl.CostEstimate(flops=flops, bytes_accessed=flops // 64, transcendentals=0),
    )(noise, *values)


STEP = 64
TILES = 5


def pair_kernel(rows, feats, places, index_ref, *refs):
    early_refs, late_ref, refs = (refs[:4], refs[4:8]), refs[8], refs[9:]
    pieces, refs = refs[: len(places)], refs[len(places):]
    targets_ref, potential_ref, blocks, held, scores, out, in_sem, out_sem = refs
    batch = 4 * rows
    eps = 2.0 / FEAT**0.5
    ln2 = math.log(2.0)
    scale = -1.0 / (FEAT * eps * ln2)
    loga = -math.log2(batch)
    own, core = index_ref[0], index_ref[1]
    half = rows // 2

    loads = []
    for k, (start, r) in enumerate(places):
        copy = pltpu.make_async_copy(
            pieces[k],
            held.at[pl.ds(start, pieces[k].shape[0]), pl.ds(r * rows, rows)],
            in_sem.at[k],
        )
        copy.start()
        loads.append(copy)

    def block(i):
        return pl.ds(pl.multiple_of(i * rows, rows), rows)

    for p in range(4):
        for side in range(2):
            into = pl.ds(pl.multiple_of((own ^ p) * rows + (core ^ side) * half, half), half)
            for r in range(DIAG):
                blocks[into, block(own ^ (p ^ r))] = early_refs[side][p][:, block(r)] * scale
        blocks[block(own ^ p), block(own ^ (p ^ DIAG))] = late_ref[block(p), :] * scale

    def sweep(_, v):
        u = []
        top = jnp.full((1, batch), -jnp.inf, jnp.float32)
        for c in range(batch // STEP):
            k = blocks[pl.ds(c * STEP, STEP), :]
            a = k + v
            m = jnp.max(a, axis=1, keepdims=True)
            s = jnp.sum(jnp.exp2(a - m), axis=1, keepdims=True)
            u.append(loga - (m + jnp.log2(s)))
            top = jnp.maximum(top, jnp.max(k + u[-1], axis=0, keepdims=True))
        total = jnp.zeros((1, batch), jnp.float32)
        for c in range(batch // STEP):
            a = blocks[pl.ds(c * STEP, STEP), :] + u[c]
            total = total + jnp.sum(jnp.exp2(a - top), axis=0, keepdims=True)
        return loga - (top + jnp.log2(total))

    v = lax.fori_loop(0, ITERS, sweep, jnp.zeros((1, batch), jnp.float32))
    potential_ref[...] = v * (eps * ln2)

    a = blocks[block(own), :] + v
    m = jnp.max(a, axis=1, keepdims=True)
    s = jnp.sum(jnp.exp2(a - m), axis=1, keepdims=True)
    scores[...] = jnp.exp2(a - (m + jnp.log2(s)))
    w = jnp.concatenate([scores[:, block(own ^ r)].T for r in range(4)], axis=0).astype(jnp.bfloat16)
    tile = feats // TILES

    def stored(t):
        part = pl.ds(pl.multiple_of(t * tile, 16), tile)
        return pltpu.make_async_copy(out.at[part, :], targets_ref.at[part, :], out_sem.at[t])

    def multiply(t, _):
        part = pl.ds(pl.multiple_of(t * tile, 16), tile)
        out[part, :] = jnp.dot(held[part, :], w, preferred_element_type=jnp.float32).astype(jnp.bfloat16)
        stored(t).start()
        return 0

    later = max(start for start, _ in places)
    for copy, (start, _) in zip(loads, places):
        if start < later:
            copy.wait()
    lax.fori_loop(0, later // tile, multiply, 0)
    for copy, (start, _) in zip(loads, places):
        if start >= later:
            copy.wait()
    lax.fori_loop(later // tile, TILES, multiply, 0)
    for t in range(TILES):
        stored(t).wait()


def paired(index, early, late, pieces, places, rows, feats):
    batch = 4 * rows
    return pl.pallas_call(
        functools.partial(pair_kernel, rows, feats, places),
        out_shape=(
            jax.ShapeDtypeStruct((feats, rows), jnp.bfloat16),
            jax.ShapeDtypeStruct((1, batch), jnp.float32),
        ),
        in_specs=[SMEM] + [VMEM] * 9 + [HBM] * len(pieces),
        out_specs=(HBM, VMEM),
        scratch_shapes=[
            pltpu.VMEM((batch, batch), jnp.float32),
            pltpu.VMEM((feats, batch), jnp.bfloat16),
            pltpu.VMEM((rows, batch), jnp.float32),
            pltpu.VMEM((feats, rows), jnp.bfloat16),
            pltpu.SemaphoreType.DMA((len(pieces),)),
            pltpu.SemaphoreType.DMA((TILES,)),
        ],
        compiler_params=pltpu.CompilerParams(vmem_limit_bytes=20 * 2**20),
        cost_estimate=pl.CostEstimate(
            flops=2 * rows * batch * feats, bytes_accessed=10 * rows * feats, transcendentals=9 * batch * batch
        ),
    )(index, *early, *late, *pieces)


def squared(values_t):
    return jnp.sum(jnp.square(values_t.astype(jnp.float32)), axis=0)


def turn(value, way):
    groups = lax.axis_size("group")
    return lax.ppermute(value, "group", [(g, g ^ way) for g in range(groups)])


def group_share(value):
    groups = lax.axis_size("group")
    rows, width = value.shape
    share = rows // groups
    parts = value.reshape(2, groups // 2, share, width).transpose(1, 0, 2, 3).reshape(rows, width)
    parts = lax.all_to_all(parts, "group", 0, 0, tiled=True)
    return jnp.sum(parts.reshape(groups, share, width), axis=0)


def line_gather(value, place):
    lines = lax.axis_size("group") // 2
    shares = jnp.stack([value] + [turn(value, 2 * way) for way in range(1, lines)])
    return jnp.concatenate(
        [lax.dynamic_index_in_dim(shares, place ^ jnp.uint32(z), keepdims=False) for z in range(lines)]
    )


def batch_swaps(value):
    return [value, swap(value, X), swap(value, Y), swap(value, DIAG)]


def local_square(noise, data):
    rows, feats = noise.shape
    noise_t, data_t = noise.T, data.T
    own, group = lax.axis_index("batch"), lax.axis_index("group").astype(jnp.uint32)
    core, line = group & 1, group >> 1
    index = jnp.stack([own.astype(jnp.int32), core.astype(jnp.int32)])

    first = feats * 8 // (15 * 128) * 128
    low, high = (0, first), (first, feats - first)
    d_low, d_high = data_t[:first], data_t[first:]
    x_all, y_low, y_high = swap(data_t, X), swap(d_low, Y), swap(d_high, Y)
    start = jnp.broadcast_to(squared(noise_t)[:, None], (rows, rows))
    own_cost = crossed(noise, (start, d_low, low, d_high, high))
    y_cost = crossed(noise, (start, y_low, low))
    y_low, own_cost, y_cost = lax.optimization_barrier((y_low, own_cost, y_cost))
    diag_low = swap(y_low, X)
    x_tail = x_all[first:]
    diag_high = swap(x_tail, Y)
    x_all, y_high, x_tail = lax.optimization_barrier((x_all, y_high, x_tail))
    early = crossed(noise, (own_cost,), (start, x_all, (0, feats)), (y_cost, y_high, high))
    early_half = line_gather(group_share(early), line)
    early_mine = batch_swaps(early_half)
    _, diag_low = lax.optimization_barrier((early_half, diag_low))
    late = crossed(noise, (start, diag_low, low))
    _, diag_high = lax.optimization_barrier((early_half, diag_high))
    late = crossed(noise, (late, diag_high, high))
    late, *early_mine = lax.optimization_barrier((late, *early_mine))
    early_rows = early_mine + [turn(value, 1) for value in early_mine]
    way = 1
    while way < lax.axis_size("group"):
        late = late + turn(late, way)
        if way == 2:
            late, *early_rows = lax.optimization_barrier((late, *early_rows))
        way *= 2
    late_rows = [jnp.concatenate(batch_swaps(late))]

    pieces = [d_low, x_all, y_low, diag_low, d_high, y_high, diag_high]
    places = [(0, 0), (0, X), (0, Y), (0, DIAG), (first, 0), (first, Y), (first, DIAG)]
    targets_t, potential = paired(index, early_rows, late_rows, pieces, places, rows, feats)
    return (targets_t.T, potential[0])


def solution(mesh):
    in_specs = (P("batch", "group"), P("batch", "group"))
    out_specs = (P("batch", "group"), P())
    groups = mesh.shape["group"]
    paired_form = mesh.shape["batch"] == 4 and groups > 1 and groups & (groups - 1) == 0
    local = local_square if paired_form else local_any
    return jax.shard_map(local, mesh=mesh, in_specs=in_specs, out_specs=out_specs, check_vma=False)
```
